1024 devices in a mesh: dp: 8 (over x, core), expert: 64 (over z, y_lo), etp: 2 (over y_hi).
Axes of the slice: x: 4, y: 8 (y_hi: 2, y_lo: 4; y = y_hi * 4 + y_lo), z: 16, core: 2. Of those that a mesh axis runs over, the one named last changes fastest.
Arguments:
- tokens: bfloat16 [12288, 2048], P(('dp', 'expert')), may hold values from -6 to 6
- cotangent: bfloat16 [12288, 2048], P(('dp', 'expert')), may hold values from -6 to 6
- scores: float32 [8, 32, 96], P('dp'), may hold values from 0.1 to 1
- chosen: int32 [8, 32, 96], P('dp'), may hold values from 0 to 1535, as said below
- w_gate: bfloat16 [64, 2048, 3584], P('expert', None, ('dp', 'etp')), may hold values from -0.125 to 0.125
- w_up: bfloat16 [64, 2048, 3584], P('expert', None, ('dp', 'etp')), may hold values from -0.125 to 0.125
- w_down: bfloat16 [64, 3584, 2048], P('expert', ('dp', 'etp')), may hold values from -0.0625 to 0.0625
Outputs:
- grad_tokens: bfloat16 [12288, 2048], P(('dp', 'expert'), 'etp')
The draws below stay inside these ranges and needn't reach their ends.
Inputs may be any that keep to these rules, and one draw needn't show every extreme that they name: chosen[r, e] names 96 different tokens of replica r, ordered by holder (token // 24), in any order within one holder; one expert takes at most 2 tokens of one holder, in every replica some expert takes exactly 2 of some holder, and the experts take 2 * 24 entries from every holder in all.
All inputs are finite; a program needn't handle non-finite values.
Results may differ from the reference program's by a relative error of at most 0.023.
Values may be sent and summed in bfloat16 or wider, within the bound.
A program may use at most 64 MiB of HBM per device.

```python
import jax
import jax.numpy as jnp
from jax import lax

D = 2048
FF = 7168
TOK_DEV = 24
EXPERTS = 32
CAP = 96
TOKENS = 12288
N_DP = 8
N_EXPERT = 64


def draw_chosen(key, part):
    key = jax.random.fold_in(key, 7)
    holders = N_EXPERT
    experts = EXPERTS
    rows_local = TOK_DEV
    capacity = CAP

    def shuffle_one(sub_key):
        return jax.random.permutation(sub_key, rows_local).astype(jnp.int32)

    def one_replica(replica_key):
        key_start, key_order, key_tokens = jax.random.split(replica_key, 3)
        start_first = (jax.random.permutation(key_start, holders).astype(jnp.int32) % experts).astype(jnp.int32)
        reorder = jnp.concatenate([jnp.zeros((1,), jnp.int32), 1 + jax.random.permutation(key_order, holders - 1).astype(jnp.int32)])
        start_second = start_first[reorder]
        expert_ids = jnp.arange(experts, dtype=jnp.int32)

        def cover(starts):
            inside = (expert_ids[None, :] - starts[:, None]) % experts < rows_local % experts
            return rows_local // experts + inside.astype(jnp.int32)
        counts = cover(start_first) + cover(start_second)
        ends = jnp.cumsum(counts, axis=0).astype(jnp.int32)
        begins = ends - counts
        positions = jnp.arange(capacity, dtype=jnp.int32)
        source = jnp.sum((ends[:, :, None] <= positions[None, None, :]).astype(jnp.int32), axis=0)
        offset = jnp.take_along_axis(begins.T, source, axis=1)
        within = positions[None, :] - offset
        shuffles = jax.vmap(shuffle_one)(jax.random.split(key_tokens, holders * experts))
        shuffles = shuffles.reshape(holders, experts, rows_local)
        local_pick = shuffles[source, expert_ids[:, None], within]
        return (source * rows_local + local_pick).astype(jnp.int32)
    return jax.vmap(one_replica)(jax.random.split(key, N_DP))


def block_levels(own_key, shape, cuts, smallest, top_value):
    def one(dim, parts):
        steps = jax.random.uniform(jax.random.fold_in(jax.random.fold_in(own_key, 6), dim), (parts,), jnp.float32, smallest / len(cuts), top_value / len(cuts))
        return jnp.repeat(jnp.exp(steps), shape[dim] // parts).reshape((-1,) + (1,) * (len(shape) - dim - 1))

    level = one(*cuts[0])
    for cut in cuts[1:]:
        level = level * one(*cut)
    return level


def gaussian(rng, extent, spread, bound, cuts=(), kind=jnp.bfloat16):
    values = jax.random.normal(rng, extent, jnp.float32) * spread
    if len(cuts) > 0:
        values = block_levels(rng, extent, cuts, -0.22, 0.18) * values
    return jnp.clip(values, min=-bound, max=bound).astype(kind)


def setup_inputs(seed: int = 0) -> dict:
    arg_keys = jax.random.split(jax.random.key(seed), 8)
    return {
        "tokens": gaussian(arg_keys[0], (TOKENS, D), 1.0, 6.0, ((0, 512),)),
        "cotangent": gaussian(arg_keys[1], (TOKENS, D), 1.0, 6.0, ((0, 512),)),
        "scores": jnp.clip(0.1 + 0.9 * jax.random.uniform(arg_keys[2], (N_DP, EXPERTS, CAP), jnp.float32) ** block_levels(arg_keys[2], (N_DP, EXPERTS, CAP), ((0, 8),), -0.2, 0.2), 0.1, 1.0),
        "chosen": draw_chosen(jax.random.fold_in(arg_keys[7], 71), 0),
        "w_gate": gaussian(arg_keys[4], (N_EXPERT, D, FF // 2), D ** -0.5, 0.125, ((0, 64), (2, 16))),
        "w_up": gaussian(arg_keys[5], (N_EXPERT, D, FF // 2), D ** -0.5, 0.125, ((0, 64), (2, 16))),
        "w_down": gaussian(arg_keys[6], (N_EXPERT, FF // 2, D), FF ** -0.5, 0.0625, ((0, 64), (1, 16))),
    }


def reference(tokens, cotangent, scores, chosen, w_gate, w_up, w_down):
    replica_rows = N_EXPERT * TOK_DEV
    offsets = (jnp.arange(N_DP, dtype=jnp.int32) * replica_rows)[:, None]

    def both_halves(weights, expert, axis_join):
        lower = lax.dynamic_index_in_dim(weights, 2 * expert, 0, keepdims=False)
        upper = lax.dynamic_index_in_dim(weights, 2 * expert + 1, 0, keepdims=False)
        return jnp.concatenate([lower, upper], axis=axis_join)

    def expert_step(grad_total, expert):
        picked = lax.dynamic_index_in_dim(chosen, expert, 1, keepdims=False).astype(jnp.int32)
        picked = (picked + offsets).reshape(-1).astype(jnp.int32)
        x_rows = jnp.take(tokens, picked, axis=0)
        dy_rows = jnp.take(cotangent, picked, axis=0)
        gain_rows = lax.dynamic_index_in_dim(scores, expert, 1, keepdims=False).reshape(-1)
        gate_full = both_halves(w_gate, expert, 1)
        up_full = both_halves(w_up, expert, 1)
        down_full = both_halves(w_down, expert, 0)
        gate_value = jnp.dot(x_rows, gate_full, preferred_element_type=jnp.float32)
        up_value = jnp.dot(x_rows, up_full, preferred_element_type=jnp.float32)
        back_hidden = gain_rows[:, None] * jnp.dot(dy_rows, down_full.T, preferred_element_type=jnp.float32)
        sigmoid_gate = jax.nn.sigmoid(gate_value)
        up_grad = (back_hidden * gate_value * sigmoid_gate).astype(jnp.bfloat16)
        gate_grad = (back_hidden * up_value * sigmoid_gate * (1.0 + gate_value * (1.0 - sigmoid_gate))).astype(jnp.bfloat16)
        row_grad = jnp.dot(gate_grad, gate_full.T, preferred_element_type=jnp.float32)
        row_grad = row_grad + jnp.dot(up_grad, up_full.T, preferred_element_type=jnp.float32)
        return grad_total.at[picked].add(row_grad), None

    start_total = jnp.zeros((N_DP * replica_rows, D), jnp.float32)
    total, unused = lax.scan(expert_step, start_total, jnp.arange(EXPERTS, dtype=jnp.int32))
    return total.astype(jnp.bfloat16)
```

```python
import functools

import jax
import jax.numpy as jnp
from jax import lax
from jax.experimental import pallas as pl
from jax.experimental.pallas import tpu as pltpu
from jax.sharding import PartitionSpec as P

MESH = pl.DeviceIdType.MESH
SEM = pltpu.SemaphoreType.DMA
FLAT = (((1,), (1,)), ((), ()))


def exchange_kernel(holders, blocks, got, send_sem, recv_sem, own_sem):
    me = lax.axis_index("expert")
    half = holders // 2
    barrier = pltpu.get_barrier_semaphore()

    def greet(k, carry):
        peer = lax.rem(me + k, holders)
        pl.semaphore_signal(barrier, inc=1, device_id={"expert": peer}, device_id_type=MESH)
        return carry

    lax.fori_loop(1, holders, greet, 0)
    own = pltpu.make_async_copy(blocks.at[me], got.at[me], own_sem)
    own.start()
    pl.semaphore_wait(barrier, holders - 1)

    def send(peer):
        pltpu.make_async_remote_copy(
            src_ref=blocks.at[peer],
            dst_ref=got.at[me],
            send_sem=send_sem,
            recv_sem=recv_sem,
            device_id={"expert": peer},
            device_id_type=MESH,
        ).start()

    def both_ways(k, carry):
        send(lax.rem(me + k, holders))
        send(lax.rem(me + holders - k, holders))
        return carry

    lax.fori_loop(1, half, both_ways, 0)
    send(lax.rem(me + half, holders))
    own.wait()
    rest = pl.ds(0, holders - 1)
    pltpu.make_async_copy(blocks.at[rest], blocks.at[rest], send_sem).wait()
    pltpu.make_async_copy(got.at[rest], got.at[rest], recv_sem).wait()


def exchange(blocks, collective_id):
    return pl.pallas_call(
        functools.partial(exchange_kernel, blocks.shape[0]),
        out_shape=jax.ShapeDtypeStruct(blocks.shape, blocks.dtype),
        in_specs=[pl.BlockSpec(memory_space=pl.ANY)],
        out_specs=pl.BlockSpec(memory_space=pl.ANY),
        scratch_shapes=[SEM, SEM, SEM],
        compiler_params=pltpu.CompilerParams(collective_id=collective_id, has_side_effects=True),
    )(blocks)


def expert_kernel(
    n_dp,
    block,
    gain,
    gate_in,
    up_in,
    down_in,
    out,
    rows,
    w_gate,
    w_up,
    w_down,
    hidden,
    part,
    total,
    direct_out,
    direct_in,
    relay_out,
    relay_in,
    sum_out,
    sum_in,
    pair_out,
    pair_in,
    half_out,
    half_in,
    w_own,
    w_send,
    w_recv,
    own_sem,
    y_sem,
    x_send,
    x_recv,
    f_send,
    f_recv,
    d_send,
    d_recv,
    r_send,
    r_recv,
    s_send,
    s_recv,
    p_sem,
    h_sem,
):
    width = rows.shape[3]
    half = width // 2
    quarter = width // 4
    dp = lax.axis_index("dp")
    holder = lax.axis_index("expert")
    etp = lax.axis_index("etp")
    q = lax.rem(holder, 2)
    core = {"dp": dp + 1 - 2 * lax.rem(dp, 2)}
    right = {"dp": lax.rem(dp + 2, n_dp)}
    left = {"dp": lax.rem(dp + n_dp - 2, n_dp)}
    pair = {"expert": holder + 1 - 2 * q}
    other = {"etp": 1 - etp}
    first, second = pl.ds(0, half), pl.ds(half, half)

    def remote(src, dst, send_sem, recv_sem, where):
        return pltpu.make_async_remote_copy(
            src_ref=src,
            dst_ref=dst,
            send_sem=send_sem,
            recv_sem=recv_sem,
            device_id=where,
            device_id_type=MESH,
        )

    own_weights = [
        pltpu.make_async_copy(src.at[0], dst.at[0], w_own.at[i])
        for i, (src, dst) in enumerate(((gate_in, w_gate), (up_in, w_up), (down_in, w_down)))
    ]
    own_block = pltpu.make_async_copy(block, rows.at[q, 0], own_sem)
    barrier = pltpu.get_barrier_semaphore()
    for peer in (core, right, left, pair, other):
        pl.semaphore_signal(barrier, inc=1, device_id=peer, device_id_type=MESH)
    own_block.start()
    for copy in own_weights:
        copy.start()
    pl.semaphore_wait(barrier, 5)

    swap = remote(block, rows.at[q, 0], y_sem.at[0], y_sem.at[1], pair)
    swap.start()

    def spread(src, kind):
        return (
            remote(src, rows.at[kind, 1], x_send.at[kind, 0], x_recv.at[kind, 0], right),
            remote(src, rows.at[kind, 2], x_send.at[kind, 1], x_recv.at[kind, 1], left),
        )

    def forward(kind):
        return (
            remote(
                rows.at[kind, 1, :, first],
                rows.at[kind, 3, :, first],
                f_send.at[kind, 0],
                f_recv.at[kind, 0],
                right,
            ),
            remote(
                rows.at[kind, 2, :, second],
                rows.at[kind, 3, :, second],
                f_send.at[kind, 1],
                f_recv.at[kind, 1],
                left,
            ),
        )

    spread_own = spread(block, q)
    for copy in spread_own:
        copy.start()
    given_weights = [
        remote(src.at[0], dst.at[1], w_send.at[i], w_recv.at[i], core)
        for i, (src, dst) in enumerate(((gate_in, w_gate), (up_in, w_up), (down_in, w_down)))
    ]
    for copy in given_weights:
        copy.start()
    swap.wait_recv()
    spread_other = spread(rows.at[1 - q, 0], 1 - q)
    for copy in spread_other:
        copy.start()
    forward_own = forward(q)
    forward_other = forward(1 - q)
    for arrive, copy in zip(spread_own, forward_own):
        arrive.wait_recv()
        copy.start()
    own_block.wait()
    for copy in own_weights:
        copy.wait()
    for copy in given_weights:
        copy.wait()

    def compute(b):
        def hidden_of(w, carry):
            x = rows[0, b]
            gate = jnp.dot(x, w_gate[w], preferred_element_type=jnp.float32)
            up = jnp.dot(x, w_up[w], preferred_element_type=jnp.float32)
            back = lax.dot_general(rows[1, b], w_down[w], FLAT, preferred_element_type=jnp.float32)
            s = jax.nn.sigmoid(gate)
            hidden[w, 0] = (back * up * s * (1.0 + gate * (1.0 - s))).astype(jnp.bfloat16)
            hidden[w, 1] = (back * gate * s).astype(jnp.bfloat16)
            return carry

        lax.fori_loop(0, 2, hidden_of, 0)

        def rows_of(n, carry):
            at = pl.ds(pl.multiple_of(n * quarter, quarter), quarter)
            grad = jnp.zeros((rows.shape[2], quarter), jnp.float32)
            for w in range(2):
                grad += lax.dot_general(
                    hidden[w, 0], w_gate[w, at, :], FLAT, preferred_element_type=jnp.float32
                )
                grad += lax.dot_general(
                    hidden[w, 1], w_up[w, at, :], FLAT, preferred_element_type=jnp.float32
                )
            part[b, n] = grad
            return carry

        lax.fori_loop(0, 4, rows_of, 0)

    def pick(b, start):
        return jnp.concatenate([part[b, start], part[b, start + 1]], axis=1)

    compute(0)
    for arrive, copy in zip(spread_other, forward_other):
        arrive.wait_recv()
        copy.start()

    compute(2)
    direct_out[0] = pick(2, 2).astype(jnp.bfloat16)
    direct_right = remote(direct_out.at[0], direct_in.at[0], d_send.at[0], d_recv.at[0], right)
    direct_right.start()
    compute(1)
    direct_out[1] = pick(1, 0).astype(jnp.bfloat16)
    direct_left = remote(direct_out.at[1], direct_in.at[1], d_send.at[1], d_recv.at[1], left)
    direct_left.start()
    for copy in forward_own + forward_other:
        copy.wait_recv()
    compute(3)
    relay_out[0] = pick(3, 0).astype(jnp.bfloat16)
    relay_right = remote(relay_out.at[0], relay_in.at[0], r_send.at[0], r_recv.at[0], right)
    relay_right.start()
    relay_out[1] = pick(3, 2).astype(jnp.bfloat16)
    relay_left = remote(relay_out.at[1], relay_in.at[1], r_send.at[1], r_recv.at[1], left)
    relay_left.start()
    relay_right.wait_recv()
    sum_out[0] = (pick(2, 0) + relay_in[0].astype(jnp.float32)).astype(jnp.bfloat16)
    sum_right = remote(sum_out.at[0], sum_in.at[0], s_send.at[0], s_recv.at[0], right)
    sum_right.start()
    relay_left.wait_recv()
    sum_out[1] = (pick(1, 2) + relay_in[1].astype(jnp.float32)).astype(jnp.bfloat16)
    sum_left = remote(sum_out.at[1], sum_in.at[1], s_send.at[1], s_recv.at[1], left)
    sum_left.start()
    direct_right.wait_recv()
    direct_left.wait_recv()
    sum_right.wait_recv()
    sum_left.wait_recv()
    weight = gain[...]
    first_half = pick(0, 0) + sum_in[0].astype(jnp.float32) + direct_in[1].astype(jnp.float32)
    second_half = pick(0, 2) + sum_in[1].astype(jnp.float32) + direct_in[0].astype(jnp.float32)
    first_half *= weight
    second_half *= weight
    total[0] = first_half[:, :quarter]
    total[1] = first_half[:, quarter:]
    total[2] = second_half[:, :quarter]
    total[3] = second_half[:, quarter:]

    pair_out[0] = total[1 - q].astype(jnp.bfloat16)
    pair_out[1] = total[3 - q].astype(jnp.bfloat16)
    pair_swap = remote(pair_out, pair_in, p_sem.at[0], p_sem.at[1], pair)
    pair_swap.start()
    pair_swap.wait_recv()
    away = total[2 * (1 - etp) + q] + pair_in[1 - etp].astype(jnp.float32)
    half_out[...] = away.astype(jnp.bfloat16)
    half_swap = remote(half_out, half_in, h_sem.at[0], h_sem.at[1], other)
    half_swap.start()
    mine = total[2 * etp + q] + pair_in[etp].astype(jnp.float32)
    half_swap.wait_recv()
    out[...] = (mine + half_in[...].astype(jnp.float32)).astype(jnp.bfloat16)
    for copy in (
        (swap, direct_right, direct_left, relay_right, relay_left, sum_right, sum_left)
        + (pair_swap, half_swap)
        + spread_own
        + spread_other
        + forward_own
        + forward_other
    ):
        copy.wait_send()


def expert_rows(n_dp, block, gain, gate, up, down):
    rows, width = block.shape
    slice_width = gate.shape[2]
    bf16, f32 = jnp.bfloat16, jnp.float32
    halves = pltpu.VMEM((2, rows, width // 2), bf16)
    any_spec = pl.BlockSpec(memory_space=pl.ANY)
    vmem_spec = pl.BlockSpec(memory_space=pltpu.VMEM)
    return pl.pallas_call(
        functools.partial(expert_kernel, n_dp),
        out_shape=jax.ShapeDtypeStruct((rows, width // 4), bf16),
        in_specs=[vmem_spec, vmem_spec, any_spec, any_spec, any_spec],
        out_specs=vmem_spec,
        scratch_shapes=[
            pltpu.VMEM((2, 4, rows, width), bf16),
            pltpu.VMEM((2, width, slice_width), bf16),
            pltpu.VMEM((2, width, slice_width), bf16),
            pltpu.VMEM((2, slice_width, width), bf16),
            pltpu.VMEM((2, 2, rows, slice_width), bf16),
            pltpu.VMEM((4, 4, rows, width // 4), f32),
            pltpu.VMEM((4, rows, width // 4), f32),
            halves,
            halves,
            halves,
            halves,
            halves,
            halves,
            pltpu.VMEM((2, rows, width // 4), bf16),
            pltpu.VMEM((2, rows, width // 4), bf16),
            pltpu.VMEM((rows, width // 4), bf16),
            pltpu.VMEM((rows, width // 4), bf16),
            SEM((3,)),
            SEM((3,)),
            SEM((3,)),
            SEM,
            SEM((2,)),
            SEM((2, 2)),
            SEM((2, 2)),
            SEM((2, 2)),
            SEM((2, 2)),
            SEM((2,)),
            SEM((2,)),
            SEM((2,)),
            SEM((2,)),
            SEM((2,)),
            SEM((2,)),
            SEM((2,)),
            SEM((2,)),
        ],
        compiler_params=pltpu.CompilerParams(
            collective_id=1, has_side_effects=True, vmem_limit_bytes=40 * 1024 * 1024
        ),
    )(block, gain, gate, up, down)


def body(tokens, cotangent, scores, chosen, w_gate, w_up, w_down):
    local_rows, model_width = tokens.shape
    experts = chosen.shape[1]
    capacity = chosen.shape[2]
    holders = lax.axis_size("expert")
    most_slots = 2 * ((local_rows + experts - 1) // experts)
    holder_index = lax.axis_index("expert")
    expert_id = holder_index // 2
    pick_table = chosen[0]
    holder_of = pick_table // local_rows
    positions = jnp.arange(capacity, dtype=jnp.int32)
    slot_range = jnp.arange(most_slots, dtype=jnp.int32)
    first_slot = jnp.sum((holder_of < holder_index).astype(jnp.int32), axis=1, keepdims=True)
    slot_index = positions[None, :] - first_slot
    is_mine = holder_of == holder_index
    pick_slot = (
        is_mine[:, :, None] & (slot_index[:, :, None] == slot_range[None, None, :])
    ).astype(jnp.bfloat16)
    local_index = pick_table - holder_index * local_rows
    pick_token = (
        local_index[:, :, None] == jnp.arange(local_rows, dtype=jnp.int32)[None, None, :]
    ).astype(jnp.bfloat16)
    sender = jnp.einsum(
        "ecj,eck->ejk", pick_slot, pick_token, preferred_element_type=jnp.float32
    ).astype(jnp.bfloat16)
    own_list = lax.dynamic_index_in_dim(pick_table, expert_id, 0, keepdims=False)
    own_holder = own_list // local_rows
    ahead_count = jnp.sum((own_holder[None, :] < own_holder[:, None]).astype(jnp.int32), axis=1)
    own_slot = positions - ahead_count
    holder_range = jnp.arange(holders, dtype=jnp.int32)
    collect = (
        (own_holder[:, None, None] == holder_range[None, :, None])
        & (own_slot[:, None, None] == slot_range[None, None, :])
    ).astype(jnp.bfloat16)
    gain = lax.dynamic_index_in_dim(scores[0], expert_id, 0, keepdims=False)[:, None]

    packed = jnp.einsum(
        "ejk,qkd->eqjd",
        sender,
        jnp.stack([tokens, cotangent]),
        preferred_element_type=jnp.float32,
    ).astype(jnp.bfloat16)
    got = exchange(packed.reshape(holders, most_slots, model_width), 0)
    block = jnp.einsum("csj,sjd->cd", collect, got, preferred_element_type=jnp.float32).astype(
        jnp.bfloat16
    )
    own_result = expert_rows(lax.axis_size("dp"), block, gain, w_gate, w_up, w_down)
    returned = jnp.einsum(
        "csj,cd->sjd", collect, own_result, preferred_element_type=jnp.float32
    ).astype(jnp.bfloat16)
    arrived = exchange(returned, 2).reshape(experts, 2, most_slots, model_width // 4)
    grad_tokens = jnp.einsum(
        "ejk,eqjd->kqd", sender, arrived, preferred_element_type=jnp.float32
    )
    return grad_tokens.reshape(local_rows, model_width // 2).astype(jnp.bfloat16)


def solution(mesh):
    placed = (
        P(("dp", "expert"), None),
        P(("dp", "expert"), None),
        P("dp", None, None),
        P("dp", None, None),
        P("expert", None, ("dp", "etp")),
        P("expert", None, ("dp", "etp")),
        P("expert", ("dp", "etp"), None),
    )
    return jax.shard_map(
        body, mesh=mesh, in_specs=placed, out_specs=P(("dp", "expert"), "etp"), check_vma=False
    )
```

```python
import functools

import jax
import jax.numpy as jnp
from jax import lax
from jax.experimental import pallas as pl
from jax.experimental.pallas import tpu as pltpu
from jax.sharding import PartitionSpec as P

MESH = pl.DeviceIdType.MESH
SEM = pltpu.SemaphoreType.DMA
FLAT = (((1,), (1,)), ((), ()))


def layer_kernel(
    n_dp,
    packed,
    collect,
    collect_t,
    gain,
    gate_in,
    up_in,
    down_in,
    arrived,
    got,
    rows,
    w_gate,
    w_up,
    w_down,
    gate_up,
    hidden,
    part,
    total,
    direct_out,
    direct_in,
    relay_out,
    relay_in,
    sum_out,
    sum_in,
    pair_out,
    pair_in,
    half_out,
    half_in,
    returned,
    z_send,
    z_recv,
    z_own,
    w_own,
    w_send,
    w_recv,
    y_send,
    y_recv,
    x_send,
    x_recv,
    f_send,
    f_recv,
    d_send,
    d_recv,
    r_send,
    r_recv,
    s_send,
    s_recv,
    p_sem,
    h_sem,
    b_sem,
):
    holders = arrived.shape[0]
    count = rows.shape[3]
    half = rows.shape[4]
    quarter = half // 2
    bf16, f32 = jnp.bfloat16, jnp.float32
    dp = lax.axis_index("dp")
    me = lax.axis_index("expert")
    etp = lax.axis_index("etp")
    q = lax.rem(me, 2)
    core = {"dp": dp + 1 - 2 * lax.rem(dp, 2)}
    right = {"dp": lax.rem(dp + 2, n_dp)}
    left = {"dp": lax.rem(dp + n_dp - 2, n_dp)}
    pair = {"expert": me + 1 - 2 * q}
    other = {"etp": 1 - etp}
    weights = ((gate_in, w_gate), (up_in, w_up), (down_in, w_down))

    def remote(src, dst, send_sem, recv_sem, where):
        return pltpu.make_async_remote_copy(
            src_ref=src,
            dst_ref=dst,
            send_sem=send_sem,
            recv_sem=recv_sem,
            device_id=where,
            device_id_type=MESH,
        )

    barrier = pltpu.get_barrier_semaphore()

    def greet(k, carry):
        peer = {"expert": lax.rem(me + k, holders)}
        pl.semaphore_signal(barrier, inc=1, device_id=peer, device_id_type=MESH)
        return carry

    lax.fori_loop(1, holders, greet, 0)
    for peer in (core, right, left, other):
        pl.semaphore_signal(barrier, inc=1, device_id=peer, device_id_type=MESH)
    own_got = [
        pltpu.make_async_copy(packed.at[kind, me], got.at[kind, me], z_own.at[kind])
        for kind in range(2)
    ]
    own_weights = [
        pltpu.make_async_copy(src.at[0], dst.at[0], w_own.at[i])
        for i, (src, dst) in enumerate(weights)
    ]
    for copy in own_got + own_weights:
        copy.start()
    pl.semaphore_wait(barrier, holders + 3)

    def to_all(send):
        def both_ways(k, carry):
            send(lax.rem(me + k, holders))
            send(lax.rem(me + holders - k, holders))
            return carry

        lax.fori_loop(1, holders // 2, both_ways, 0)
        send(lax.rem(me + holders // 2, holders))

    def dispatch(kind):
        def send(peer):
            remote(
                packed.at[kind, peer],
                got.at[kind, me],
                z_send.at[kind],
                z_recv.at[kind],
                {"expert": peer},
            ).start()

        to_all(send)

    rest = pl.ds(0, holders - 1)

    def all_of(ref, sem):
        pltpu.make_async_copy(ref.at[rest], ref.at[rest], sem).wait()

    dispatch(0)
    given_weights = [
        remote(src.at[0], dst.at[1], w_send.at[i], w_recv.at[i], core)
        for i, (src, dst) in enumerate(weights)
    ]
    for copy in given_weights:
        copy.start()
    dispatch(1)

    def spread(kind, side):
        src = rows.at[kind, 0, side]
        return (
            remote(
                src,
                rows.at[kind, 1, side],
                x_send.at[kind, side, 0],
                x_recv.at[kind, side, 0],
                right,
            ),
            remote(
                src,
                rows.at[kind, 2, side],
                x_send.at[kind, side, 1],
                x_recv.at[kind, side, 1],
                left,
            ),
        )

    def forward(kind, side):
        upper, lower = pl.ds(0, count // 2), pl.ds(count // 2, count // 2)
        return (
            remote(
                rows.at[kind, 1, side, upper],
                rows.at[kind, 3, side, upper],
                f_send.at[kind, side, 0],
                f_recv.at[kind, side, 0],
                right,
            ),
            remote(
                rows.at[kind, 2, side, lower],
                rows.at[kind, 3, side, lower],
                f_send.at[kind, side, 1],
                f_recv.at[kind, side, 1],
                left,
            ),
        )

    swaps, spreads, forwards = [], {}, {}
    for kind in range(2):
        swaps.append(
            remote(
                rows.at[kind, 0, q], rows.at[kind, 0, q], y_send.at[kind], y_recv.at[kind], pair
            )
        )
        for which, side in ((0, q), (1, 1 - q)):
            spreads[kind, which] = spread(kind, side)
            forwards[kind, which] = forward(kind, side)

    def compact(kind):
        own_got[kind].wait()
        all_of(got.at[kind], z_recv.at[kind])
        slots = got[kind].reshape(2 * holders, half)
        rows[kind, 0, q] = jnp.dot(collect[...], slots, preferred_element_type=f32).astype(bf16)
        swaps[kind].start()
        for copy in spreads[kind, 0]:
            copy.start()

    def pass_on(kind, which):
        for arrive, copy in zip(spreads[kind, which], forwards[kind, which]):
            arrive.wait_recv()
            copy.start()

    def times(kind, b, n, weight):
        a = rows[kind, pl.ds(b, n), 0].reshape(n * count, half)
        c = rows[kind, pl.ds(b, n), 1].reshape(n * count, half)
        return lax.dot_general(
            a, weight[:, :half], FLAT, preferred_element_type=f32
        ) + lax.dot_general(c, weight[:, half:], FLAT, preferred_element_type=f32)

    def first_products(b, n):
        def one(w, carry):
            gate_up[0, w, pl.ds(b * count, n * count)] = times(0, b, n, w_gate[w])
            gate_up[1, w, pl.ds(b * count, n * count)] = times(0, b, n, w_up[w])
            return carry

        lax.fori_loop(0, 2, one, 0)

    def hidden_grads(b, n):
        def one(w, carry):
            back = times(1, b, n, w_down[w])
            gate = gate_up[0, w, pl.ds(b * count, n * count)]
            up = gate_up[1, w, pl.ds(b * count, n * count)]
            s = jax.nn.sigmoid(gate)
            here = pl.ds(0, n * count)
            hidden[w, 0, here] = (back * up * s * (1.0 + gate * (1.0 - s))).astype(bf16)
            hidden[w, 1, here] = (back * gate * s).astype(bf16)
            return carry

        lax.fori_loop(0, 2, one, 0)

    def row_grads(b, n, piece):
        at = pl.ds(pl.multiple_of(piece * quarter, quarter), quarter)
        here = pl.ds(0, n * count)
        grad = jnp.zeros((n * count, quarter), f32)
        for w in range(2):
            for i, weight in enumerate((w_gate, w_up)):
                grad += jnp.dot(hidden[w, i, here], weight[w, :, at], preferred_element_type=f32)
        part[pl.ds(b, n), piece] = grad.reshape(n, count, quarter)

    def all_row_grads(b, n):
        def one(piece, carry):
            row_grads(b, n, piece)
            return carry

        lax.fori_loop(0, 4, one, 0)

    compact(0)
    swaps[0].wait_recv()
    for copy in spreads[0, 1]:
        copy.start()
    pass_on(0, 0)
    for copy in own_weights + given_weights:
        copy.wait()
    first_products(0, 1)
    compact(1)
    pass_on(0, 1)
    first_products(1, 2)
    swaps[1].wait_recv()
    for copy in spreads[1, 1]:
        copy.start()
    pass_on(1, 0)
    for copy in forwards[0, 0] + forwards[0, 1]:
        copy.wait_recv()
    first_products(3, 1)
    hidden_grads(0, 1)
    all_row_grads(0, 1)
    pass_on(1, 1)

    hidden_grads(1, 2)
    all_row_grads(1, 2)
    for piece in range(2):
        direct_out[0, piece] = part[2, 2 + piece].astype(bf16)
        direct_out[1, piece] = part[1, piece].astype(bf16)
    direct = [
        remote(direct_out.at[i], direct_in.at[i], d_send.at[i], d_recv.at[i], where)
        for i, where in ((0, right), (1, left))
    ]
    for copy in direct:
        copy.start()
    for copy in forwards[1, 0] + forwards[1, 1]:
        copy.wait_recv()
    hidden_grads(3, 1)

    relays, sums = [], []
    for stage, sub in ((0, 1 - q), (1, q)):
        for i, piece, where in ((0, sub, right), (1, 2 + sub, left)):
            row_grads(3, 1, piece)
            relay_out[i, stage] = part[3, piece].astype(bf16)
            relays.append(
                remote(
                    relay_out.at[i, stage],
                    relay_in.at[i, stage],
                    r_send.at[i, stage],
                    r_recv.at[i, stage],
                    where,
                )
            )
            relays[-1].start()
    for stage, sub in ((0, 1 - q), (1, q)):
        for i, b, piece, where in ((0, 2, sub, right), (1, 1, 2 + sub, left)):
            relays[2 * stage + i].wait_recv()
            sum_out[i, stage] = (part[b, piece] + relay_in[i, stage].astype(f32)).astype(bf16)
            sums.append(
                remote(
                    sum_out.at[i, stage],
                    sum_in.at[i, stage],
                    s_send.at[i, stage],
                    s_recv.at[i, stage],
                    where,
                )
            )
            sums[-1].start()
    for copy in direct:
        copy.wait_recv()
    weight = gain[...]

    def along_x(stage, sub, i):
        sums[2 * stage + i].wait_recv()
        terms = sum_in[i, stage].astype(f32) + direct_in[1 - i, sub].astype(f32)
        return (part[0, 2 * i + sub] + terms) * weight

    for i in range(2):
        pair_out[i] = along_x(0, 1 - q, i).astype(bf16)
    pair_swap = remote(pair_out, pair_in, p_sem.at[0], p_sem.at[1], pair)
    pair_swap.start()
    for i in range(2):
        total[i] = along_x(1, q, i)
    pair_swap.wait_recv()
    half_out[...] = (total[1 - etp] + pair_in[1 - etp].astype(f32)).astype(bf16)
    half_swap = remote(half_out, half_in, h_sem.at[0], h_sem.at[1], other)
    half_swap.start()
    mine = total[etp] + pair_in[etp].astype(f32)
    half_swap.wait_recv()
    result = (mine + half_in[...].astype(f32)).astype(bf16)

    slots = jnp.dot(collect_t[...], result, preferred_element_type=f32).astype(bf16)
    returned[...] = slots.reshape(holders, 2, quarter)
    own_back = pltpu.make_async_copy(returned.at[me], arrived.at[me], b_sem.at[2])
    own_back.start()

    def send_back(peer):
        remote(
            returned.at[peer], arrived.at[me], b_sem.at[0], b_sem.at[1], {"expert": peer}
        ).start()

    to_all(send_back)
    own_back.wait()
    all_of(returned, b_sem.at[0])
    for kind in range(2):
        all_of(packed.at[kind], z_send.at[kind])
    copies = swaps + direct + relays + sums + [pair_swap, half_swap]
    for key in spreads:
        copies += spreads[key] + forwards[key]
    for copy in copies:
        copy.wait_send()
    all_of(arrived, b_sem.at[1])


def layer(n_dp, packed, collect, gain, gate, up, down):
    holders, most_slots, half = packed.shape[1:]
    count = collect.shape[0]
    quarter = half // 2
    slice_width = gate.shape[1]
    bf16, f32 = jnp.bfloat16, jnp.float32
    any_spec = pl.BlockSpec(memory_space=pl.ANY)
    vmem_spec = pl.BlockSpec(memory_space=pltpu.VMEM)
    slices = pltpu.VMEM((2, slice_width, 2 * half), bf16)
    quarters = pltpu.VMEM((2, 2, count, quarter), bf16)
    two_quarters = pltpu.VMEM((2, count, quarter), bf16)
    one_quarter = pltpu.VMEM((count, quarter), bf16)
    return pl.pallas_call(
        functools.partial(layer_kernel, n_dp),
        out_shape=jax.ShapeDtypeStruct((holders, most_slots, quarter), bf16),
        in_specs=[any_spec, vmem_spec, vmem_spec, vmem_spec, any_spec, any_spec, any_spec],
        out_specs=any_spec,
        scratch_shapes=[
            pltpu.VMEM((2, holders, most_slots, half), bf16),
            pltpu.VMEM((2, 4, 2, count, half), bf16),
            slices,
            slices,
            slices,
            pltpu.VMEM((2, 2, 4 * count, slice_width), f32),
            pltpu.VMEM((2, 2, 2 * count, slice_width), bf16),
            pltpu.VMEM((4, 4, count, quarter), f32),
            pltpu.VMEM((2, count, quarter), f32),
            quarters,
            quarters,
            quarters,
            quarters,
            quarters,
            quarters,
            two_quarters,
            two_quarters,
            one_quarter,
            one_quarter,
            pltpu.VMEM((holders, most_slots, quarter), bf16),
            SEM((2,)),
            SEM((2,)),
            SEM((2,)),
            SEM((3,)),
            SEM((3,)),
            SEM((3,)),
            SEM((2,)),
            SEM((2,)),
            SEM((2, 2, 2)),
            SEM((2, 2, 2)),
            SEM((2, 2, 2)),
            SEM((2, 2, 2)),
            SEM((2,)),
            SEM((2,)),
            SEM((2, 2)),
            SEM((2, 2)),
            SEM((2, 2)),
            SEM((2, 2)),
            SEM((2,)),
            SEM((2,)),
            SEM((3,)),
        ],
        compiler_params=pltpu.CompilerParams(
            collective_id=0, has_side_effects=True, vmem_limit_bytes=40 * 1024 * 1024
        ),
    )(packed, collect, collect.T, gain, gate, up, down)


def body(tokens, cotangent, scores, chosen, w_gate, w_up, w_down):
    local_rows, model_width = tokens.shape
    experts = chosen.shape[1]
    capacity = chosen.shape[2]
    holders = lax.axis_size("expert")
    most_slots = 2 * ((local_rows + experts - 1) // experts)
    holder_index = lax.axis_index("expert")
    expert_id = holder_index // 2
    pick_table = chosen[0]
    holder_of = pick_table // local_rows
    positions = jnp.arange(capacity, dtype=jnp.int32)
    slot_range = jnp.arange(most_slots, dtype=jnp.int32)
    first_slot = jnp.sum((holder_of < holder_index).astype(jnp.int32), axis=1, keepdims=True)
    slot_index = positions[None, :] - first_slot
    is_mine = holder_of == holder_index
    pick_slot = (
        is_mine[:, :, None] & (slot_index[:, :, None] == slot_range[None, None, :])
    ).astype(jnp.bfloat16)
    local_index = pick_table - holder_index * local_rows
    pick_token = (
        local_index[:, :, None] == jnp.arange(local_rows, dtype=jnp.int32)[None, None, :]
    ).astype(jnp.bfloat16)
    sender = jnp.einsum(
        "ecj,eck->ejk", pick_slot, pick_token, preferred_element_type=jnp.float32
    ).astype(jnp.bfloat16)
    own_list = lax.dynamic_index_in_dim(pick_table, expert_id, 0, keepdims=False)
    own_holder = own_list // local_rows
    ahead_count = jnp.sum((own_holder[None, :] < own_holder[:, None]).astype(jnp.int32), axis=1)
    own_slot = positions - ahead_count
    holder_range = jnp.arange(holders, dtype=jnp.int32)
    collect = (
        (own_holder[:, None, None] == holder_range[None, :, None])
        & (own_slot[:, None, None] == slot_range[None, None, :])
    ).astype(jnp.bfloat16)
    gain = lax.dynamic_index_in_dim(scores[0], expert_id, 0, keepdims=False)[:, None]

    stacked = jnp.stack([tokens, cotangent]).reshape(2, local_rows, 2, model_width // 2)
    packed = jnp.einsum(
        "ejk,akqd->aeqjd", sender, stacked, preferred_element_type=jnp.float32
    ).astype(jnp.bfloat16)
    arrived = layer(
        lax.axis_size("dp"),
        packed.reshape(2, holders, most_slots, model_width // 2),
        collect.reshape(capacity, holders * most_slots),
        gain,
        jnp.swapaxes(w_gate, 1, 2),
        jnp.swapaxes(w_up, 1, 2),
        w_down,
    ).reshape(experts, 2, most_slots, model_width // 4)
    grad_tokens = jnp.einsum(
        "ejk,eqjd->kqd", sender, arrived, preferred_element_type=jnp.float32
    )
    return grad_tokens.reshape(local_rows, model_width // 2).astype(jnp.bfloat16)


def solution(mesh):
    placed = (
        P(("dp", "expert"), None),
        P(("dp", "expert"), None),
        P("dp", None, None),
        P("dp", None, None),
        P("expert", None, ("dp", "etp")),
        P("expert", None, ("dp", "etp")),
        P("expert", ("dp", "etp"), None),
    )
    return jax.shard_map(
        body, mesh=mesh, in_specs=placed, out_specs=P(("dp", "expert"), "etp"), check_vma=False
    )
```

```python
import functools

import jax
import jax.numpy as jnp
from jax import lax
from jax.experimental import pallas as pl
from jax.experimental.pallas import tpu as pltpu
from jax.sharding import PartitionSpec as P

MESH = pl.DeviceIdType.MESH
SEM = pltpu.SemaphoreType.DMA
FLAT = (((1,), (1,)), ((), ()))


def layer_kernel(
    n_dp,
    packed,
    collect,
    collect_t,
    gain,
    gate_in,
    up_in,
    down_in,
    arrived,
    got,
    rows,
    w_gate,
    w_up,
    w_down,
    gate_up,
    hidden,
    part,
    total,
    direct_out,
    direct_in,
    relay_out,
    relay_in,
    sum_out,
    sum_in,
    pair_out,
    pair_in,
    half_out,
    half_in,
    returned,
    z_send,
    z_recv,
    z_own,
    w_own,
    w_send,
    w_recv,
    y_send,
    y_recv,
    o_sem,
    x_send,
    x_recv,
    f_send,
    f_recv,
    d_send,
    d_recv,
    r_send,
    r_recv,
    s_send,
    s_recv,
    p_send,
    p_recv,
    h_sem,
    b_sem,
):
    holders = arrived.shape[0]
    count = rows.shape[3]
    quarter = rows.shape[4]
    upper, lower = pl.ds(0, count // 2), pl.ds(count // 2, count // 2)
    bf16, f32 = jnp.bfloat16, jnp.float32
    dp = lax.axis_index("dp")
    me = lax.axis_index("expert")
    etp = lax.axis_index("etp")
    q = lax.rem(me, 2)
    core = {"dp": dp + 1 - 2 * lax.rem(dp, 2)}
    right = {"dp": lax.rem(dp + 2, n_dp)}
    left = {"dp": lax.rem(dp + n_dp - 2, n_dp)}
    pair = {"expert": me + 1 - 2 * q}
    other = {"etp": 1 - etp}
    chunks = ((0, etp), (1, etp), (1, 1 - etp), (0, 1 - etp))
    weights = ((gate_in, w_gate), (up_in, w_up), (down_in, w_down))

    def remote(src, dst, send_sem, recv_sem, where):
        return pltpu.make_async_remote_copy(
            src_ref=src,
            dst_ref=dst,
            send_sem=send_sem,
            recv_sem=recv_sem,
            device_id=where,
            device_id_type=MESH,
        )

    barrier = pltpu.get_barrier_semaphore()

    def greet(k, carry):
        peer = {"expert": lax.rem(me + k, holders)}
        pl.semaphore_signal(barrier, inc=1, device_id=peer, device_id_type=MESH)
        return carry

    lax.fori_loop(1, holders, greet, 0)
    for peer in (core, right, left, other):
        pl.semaphore_signal(barrier, inc=1, device_id=peer, device_id_type=MESH)
    own_got = [
        pltpu.make_async_copy(packed.at[kind, p, me], got.at[c, me], z_own.at[c])
        for c, (kind, p) in enumerate(chunks[:3])
    ]
    own_weights = [
        pltpu.make_async_copy(src.at[0], dst.at[0], w_own.at[i])
        for i, (src, dst) in enumerate(weights)
    ]
    for copy in own_got + own_weights:
        copy.start()
    pl.semaphore_wait(barrier, holders + 3)

    def to_all(send):
        def both_ways(k, carry):
            send(lax.rem(me + k, holders))
            send(lax.rem(me + holders - k, holders))
            return carry

        lax.fori_loop(1, holders // 2, both_ways, 0)
        send(lax.rem(me + holders // 2, holders))

    def dispatch(c):
        kind, p = chunks[c]

        def send(peer):
            remote(
                packed.at[kind, p, peer],
                got.at[c, me],
                z_send.at[c],
                z_recv.at[c],
                {"expert": peer},
            ).start()

        to_all(send)

    rest = pl.ds(0, holders - 1)

    def all_of(ref, sem):
        pltpu.make_async_copy(ref.at[rest], ref.at[rest], sem).wait()

    dispatch(0)
    given_weights = [
        remote(src.at[0], dst.at[1], w_send.at[i], w_recv.at[i], core)
        for i, (src, dst) in enumerate(weights)
    ]
    for copy in given_weights:
        copy.start()
    dispatch(1)

    def spread(c, which):
        kind, p = chunks[c]
        at = 2 * (q if which == 0 else 1 - q) + p
        src = rows.at[kind, 0, at]
        return tuple(
            remote(
                src,
                rows.at[kind, 1 + i, at],
                x_send.at[c, which, i],
                x_recv.at[c, which, i],
                where,
            )
            for i, where in ((0, right), (1, left))
        )

    def forward(c, which):
        kind, p = chunks[c]
        at = 2 * (q if which == 0 else 1 - q) + p
        return tuple(
            remote(
                rows.at[kind, 1 + i, at, part_of],
                rows.at[kind, 3, at, part_of],
                f_send.at[c, which, i],
                f_recv.at[c, which, i],
                where,
            )
            for i, part_of, where in ((0, upper, right), (1, lower, left))
        )

    swaps, spreads, forwards = [], {}, {}
    for c, (kind, p) in enumerate(chunks):
        mine = rows.at[kind, 0, 2 * q + p]
        swaps.append(remote(mine, mine, y_send.at[c], y_recv.at[c], pair))
        for which in range(2):
            spreads[c, which] = spread(c, which)
            forwards[c, which] = forward(c, which)
    crossed = rows.at[0, 0, 2 * q + etp]
    cross = remote(crossed, crossed, o_sem.at[0], o_sem.at[1], other)

    def send_own(c):
        swaps[c].start()
        for copy in spreads[c, 0]:
            copy.start()

    def compact(c):
        kind, p = chunks[c]
        own_got[c].wait()
        all_of(got.at[c], z_recv.at[c])
        slots = got[c].reshape(2 * holders, quarter)
        dense = jnp.dot(collect[...], slots, preferred_element_type=f32)
        rows[kind, 0, 2 * q + p] = dense.astype(bf16)

    def send_pairs(c):
        swaps[c].wait_recv()
        for copy in spreads[c, 1]:
            copy.start()

    def pass_on(c, which):
        for arrive, copy in zip(spreads[c, which], forwards[c, which]):
            arrive.wait_recv()
            copy.start()

    def passed(c):
        for copy in forwards[c, 0] + forwards[c, 1]:
            copy.wait_recv()

    def times(kind, b, n, weight):
        total_of = jnp.zeros((n * count, weight.shape[0]), f32)
        for piece in range(4):
            a = rows[kind, pl.ds(b, n), piece].reshape(n * count, quarter)
            columns = weight[:, piece * quarter : (piece + 1) * quarter]
            total_of += lax.dot_general(a, columns, FLAT, preferred_element_type=f32)
        return total_of

    def first_products(b, n):
        def one(w, carry):
            gate_up[0, w, pl.ds(b * count, n * count)] = times(0, b, n, w_gate[w])
            gate_up[1, w, pl.ds(b * count, n * count)] = times(0, b, n, w_up[w])
            return carry

        lax.fori_loop(0, 2, one, 0)

    def hidden_grads(b, n):
        def one(w, carry):
            back = times(1, b, n, w_down[w])
            gate = gate_up[0, w, pl.ds(b * count, n * count)]
            up = gate_up[1, w, pl.ds(b * count, n * count)]
            s = jax.nn.sigmoid(gate)
            here = pl.ds(0, n * count)
            hidden[w, 0, here] = (back * up * s * (1.0 + gate * (1.0 - s))).astype(bf16)
            hidden[w, 1, here] = (back * gate * s).astype(bf16)
            return carry

        lax.fori_loop(0, 2, one, 0)

    def row_grads(b, n, piece):
        at = pl.ds(pl.multiple_of(piece * quarter, quarter), quarter)
        here = pl.ds(0, n * count)
        grad = jnp.zeros((n * count, quarter), f32)
        for w in range(2):
            for i, weight in enumerate((w_gate, w_up)):
                grad += jnp.dot(hidden[w, i, here], weight[w, :, at], preferred_element_type=f32)
        part[pl.ds(b, n), piece] = grad.reshape(n, count, quarter)

    def all_row_grads(b, n):
        def one(piece, carry):
            row_grads(b, n, piece)
            return carry

        lax.fori_loop(0, 4, one, 0)

    compact(0)
    cross.start()
    send_own(0)
    dispatch(2)
    send_pairs(0)
    pass_on(0, 0)
    compact(1)
    send_own(1)
    pass_on(0, 1)
    cross.wait_recv()
    send_own(3)
    send_pairs(1)
    pass_on(1, 0)
    compact(2)
    send_own(2)
    pass_on(1, 1)
    send_pairs(3)
    pass_on(3, 0)
    send_pairs(2)
    pass_on(2, 0)
    for copy in own_weights + given_weights:
        copy.wait()
    first_products(0, 1)
    pass_on(3, 1)
    first_products(1, 2)
    hidden_grads(0, 1)
    pass_on(2, 1)
    all_row_grads(0, 1)
    passed(0)
    passed(3)
    first_products(3, 1)

    hidden_grads(1, 2)
    all_row_grads(1, 2)
    direct_out[0] = part[2, :, lower].astype(bf16)
    direct_out[1] = part[1, :, upper].astype(bf16)
    direct = [
        remote(direct_out.at[i], direct_in.at[i], d_send.at[i], d_recv.at[i], where)
        for i, where in ((0, right), (1, left))
    ]
    for copy in direct:
        copy.start()
    passed(1)
    passed(2)
    hidden_grads(3, 1)

    order = (2 * (1 - etp) + 1 - q, 2 * (1 - etp) + q, 2 * etp + 1 - q, 2 * etp + q)
    relays, sums = [], []
    for stage, piece in enumerate(order):
        row_grads(3, 1, piece)
        for i, part_of, where in ((0, upper, right), (1, lower, left)):
            relay_out[i, stage] = part[3, piece, part_of].astype(bf16)
            relays.append(
                remote(
                    relay_out.at[i, stage],
                    relay_in.at[i, stage],
                    r_send.at[i, stage],
                    r_recv.at[i, stage],
                    where,
                )
            )
            relays[-1].start()
    for stage, piece in enumerate(order):
        for i, b, part_of, where in ((0, 2, upper, right), (1, 1, lower, left)):
            relays[2 * stage + i].wait_recv()
            added = part[b, piece, part_of] + relay_in[i, stage].astype(f32)
            sum_out[i, stage] = added.astype(bf16)
            sums.append(
                remote(
                    sum_out.at[i, stage],
                    sum_in.at[i, stage],
                    s_send.at[i, stage],
                    s_recv.at[i, stage],
                    where,
                )
            )
            sums[-1].start()
    for copy in direct:
        copy.wait_recv()

    def along_x(stage):
        piece = order[stage]
        pieces = []
        for i, part_of in ((0, upper), (1, lower)):
            sums[2 * stage + i].wait_recv()
            terms = sum_in[i, stage].astype(f32) + direct_in[1 - i, piece].astype(f32)
            pieces.append((part[0, piece, part_of] + terms) * gain[part_of, :])
        return jnp.concatenate(pieces, axis=0)

    pair_swaps = [
        remote(pair_out.at[i], pair_in.at[i], p_send.at[i], p_recv.at[i], pair) for i in range(2)
    ]
    pair_out[0] = along_x(0).astype(bf16)
    pair_swaps[0].start()
    total[...] = along_x(1)
    pair_swaps[0].wait_recv()
    half_out[...] = (total[...] + pair_in[0].astype(f32)).astype(bf16)
    half_swap = remote(half_out, half_in, h_sem.at[0], h_sem.at[1], other)
    half_swap.start()
    pair_out[1] = along_x(2).astype(bf16)
    pair_swaps[1].start()
    total[...] = along_x(3)
    pair_swaps[1].wait_recv()
    total[...] += pair_in[1].astype(f32)
    half_swap.wait_recv()
    result = (total[...] + half_in[...].astype(f32)).astype(bf16)

    slots = jnp.dot(collect_t[...], result, preferred_element_type=f32).astype(bf16)
    returned[...] = slots.reshape(holders, 2, quarter)
    own_back = pltpu.make_async_copy(returned.at[me], arrived.at[me], b_sem.at[2])
    own_back.start()

    def send_back(peer):
        remote(
            returned.at[peer], arrived.at[me], b_sem.at[0], b_sem.at[1], {"expert": peer}
        ).start()

    to_all(send_back)
    own_back.wait()
    all_of(returned, b_sem.at[0])
    for c, (kind, p) in enumerate(chunks[:3]):
        all_of(packed.at[kind, p], z_send.at[c])
    copies = swaps + direct + relays + sums + pair_swaps + [cross, half_swap]
    for key in spreads:
        copies += spreads[key] + forwards[key]
    for copy in copies:
        copy.wait_send()
    all_of(arrived, b_sem.at[1])


def layer(n_dp, packed, collect, gain, gate, up, down):
    holders, most_slots, quarter = packed.shape[2:]
    count = collect.shape[0]
    slice_width = gate.shape[1]
    bf16, f32 = jnp.bfloat16, jnp.float32
    any_spec = pl.BlockSpec(memory_space=pl.ANY)
    vmem_spec = pl.BlockSpec(memory_space=pltpu.VMEM)
    slices = pltpu.VMEM((2, slice_width, 4 * quarter), bf16)
    half_rows = pltpu.VMEM((2, 4, count // 2, quarter), bf16)
    two_quarters = pltpu.VMEM((2, count, quarter), bf16)
    one_quarter = pltpu.VMEM((count, quarter), bf16)
    return pl.pallas_call(
        functools.partial(layer_kernel, n_dp),
        out_shape=jax.ShapeDtypeStruct((holders, most_slots, quarter), bf16),
        in_specs=[any_spec, vmem_spec, vmem_spec, vmem_spec, any_spec, any_spec, any_spec],
        out_specs=any_spec,
        scratch_shapes=[
            pltpu.VMEM((3, holders, most_slots, quarter), bf16),
            pltpu.VMEM((2, 4, 4, count, quarter), bf16),
            slices,
            slices,
            slices,
            pltpu.VMEM((2, 2, 4 * count, slice_width), f32),
            pltpu.VMEM((2, 2, 2 * count, slice_width), bf16),
            pltpu.VMEM((4, 4, count, quarter), f32),
            pltpu.VMEM((count, quarter), f32),
            half_rows,
            half_rows,
            half_rows,
            half_rows,
            half_rows,
            half_rows,
            two_quarters,
            two_quarters,
            one_quarter,
            one_quarter,
            pltpu.VMEM((holders, most_slots, quarter), bf16),
            SEM((3,)),
            SEM((3,)),
            SEM((3,)),
            SEM((3,)),
            SEM((3,)),
            SEM((3,)),
            SEM((4,)),
            SEM((4,)),
            SEM((2,)),
            SEM((4, 2, 2)),
            SEM((4, 2, 2)),
            SEM((4, 2, 2)),
            SEM((4, 2, 2)),
            SEM((2,)),
            SEM((2,)),
            SEM((2, 4)),
            SEM((2, 4)),
            SEM((2, 4)),
            SEM((2, 4)),
            SEM((2,)),
            SEM((2,)),
            SEM((2,)),
            SEM((3,)),
        ],
        compiler_params=pltpu.CompilerParams(
            collective_id=0, has_side_effects=True, vmem_limit_bytes=40 * 1024 * 1024
        ),
    )(packed, collect, collect.T, gain, gate, up, down)


def body(tokens, cotangent, scores, chosen, w_gate, w_up, w_down):
    local_rows, model_width = tokens.shape
    experts = chosen.shape[1]
    capacity = chosen.shape[2]
    holders = lax.axis_size("expert")
    most_slots = 2 * ((local_rows + experts - 1) // experts)
    holder_index = lax.axis_index("expert")
    expert_id = holder_index // 2
    pick_table = chosen[0]
    holder_of = pick_table // local_rows
    positions = jnp.arange(capacity, dtype=jnp.int32)
    slot_range = jnp.arange(most_slots, dtype=jnp.int32)
    first_slot = jnp.sum((holder_of < holder_index).astype(jnp.int32), axis=1, keepdims=True)
    slot_index = positions[None, :] - first_slot
    is_mine = holder_of == holder_index
    pick_slot = (
        is_mine[:, :, None] & (slot_index[:, :, None] == slot_range[None, None, :])
    ).astype(jnp.bfloat16)
    local_index = pick_table - holder_index * local_rows
    pick_token = (
        local_index[:, :, None] == jnp.arange(local_rows, dtype=jnp.int32)[None, None, :]
    ).astype(jnp.bfloat16)
    sender = jnp.einsum(
        "ecj,eck->ejk", pick_slot, pick_token, preferred_element_type=jnp.float32
    ).astype(jnp.bfloat16)
    own_list = lax.dynamic_index_in_dim(pick_table, expert_id, 0, keepdims=False)
    own_holder = own_list // local_rows
    ahead_count = jnp.sum((own_holder[None, :] < own_holder[:, None]).astype(jnp.int32), axis=1)
    own_slot = positions - ahead_count
    holder_range = jnp.arange(holders, dtype=jnp.int32)
    collect = (
        (own_holder[:, None, None] == holder_range[None, :, None])
        & (own_slot[:, None, None] == slot_range[None, None, :])
    ).astype(jnp.bfloat16)
    gain = lax.dynamic_index_in_dim(scores[0], expert_id, 0, keepdims=False)[:, None]

    stacked = jnp.stack([tokens, cotangent]).reshape(2, local_rows, 2, 2, model_width // 4)
    packed = jnp.einsum(
        "ejk,akqpd->apeqjd", sender, stacked, preferred_element_type=jnp.float32
    ).astype(jnp.bfloat16)
    arrived = layer(
        lax.axis_size("dp"),
        packed.reshape(2, 2, holders, most_slots, model_width // 4),
        collect.reshape(capacity, holders * most_slots),
        gain,
        jnp.swapaxes(w_gate, 1, 2),
        jnp.swapaxes(w_up, 1, 2),
        w_down,
    ).reshape(experts, 2, most_slots, model_width // 4)
    grad_tokens = jnp.einsum(
        "ejk,eqjd->kqd", sender, arrived, preferred_element_type=jnp.float32
    )
    return grad_tokens.reshape(local_rows, model_width // 2).astype(jnp.bfloat16)


def solution(mesh):
    placed = (
        P(("dp", "expert"), None),
        P(("dp", "expert"), None),
        P("dp", None, None),
        P("dp", None, None),
        P("expert", None, ("dp", "etp")),
        P("expert", None, ("dp", "etp")),
        P("expert", ("dp", "etp"), None),
    )
    return jax.shard_map(
        body, mesh=mesh, in_specs=placed, out_specs=P(("dp", "expert"), "etp"), check_vma=False
    )
```

```python
import functools

import jax
import jax.numpy as jnp
from jax import lax
from jax.experimental import pallas as pl
from jax.experimental.pallas import tpu as pltpu
from jax.sharding import PartitionSpec as P

MESH = pl.DeviceIdType.MESH
SEM = pltpu.SemaphoreType.DMA
FLAT = (((1,), (1,)), ((), ()))


def layer_kernel(
    n_dp,
    packed,
    collect,
    collect_t,
    gain,
    gate_in,
    up_in,
    down_in,
    arrived,
    got,
    rows,
    w_gate,
    w_up,
    w_down,
    gate_up,
    hidden,
    part,
    total,
    direct_out,
    direct_in,
    relay_out,
    relay_in,
    sum_out,
    sum_in,
    pair_out,
    pair_in,
    half_out,
    half_in,
    returned,
    z_send,
    z_recv,
    z_own,
    w_own,
    w_send,
    w_recv,
    y_send,
    y_recv,
    o_sem,
    l_send,
    l_recv,
    x_send,
    x_recv,
    f_send,
    f_recv,
    d_send,
    d_recv,
    r_send,
    r_recv,
    s_send,
    s_recv,
    p_send,
    p_recv,
    h_sem,
    b_sem,
):
    holders = arrived.shape[0]
    count = rows.shape[3]
    quarter = rows.shape[4]
    upper, lower = pl.ds(0, count // 2), pl.ds(count // 2, count // 2)
    bf16, f32 = jnp.bfloat16, jnp.float32
    dp = lax.axis_index("dp")
    me = lax.axis_index("expert")
    etp = lax.axis_index("etp")
    q = lax.rem(me, 2)
    core = {"dp": dp + 1 - 2 * lax.rem(dp, 2)}
    right = {"dp": lax.rem(dp + 2, n_dp)}
    left = {"dp": lax.rem(dp + n_dp - 2, n_dp)}
    pair = {"expert": me + 1 - 2 * q}
    other = {"etp": 1 - etp}
    chunks = ((0, etp), (1, etp), (1, 1 - etp), (0, 1 - etp))
    weights = ((gate_in, w_gate), (up_in, w_up), (down_in, w_down))

    def remote(src, dst, send_sem, recv_sem, where):
        return pltpu.make_async_remote_copy(
            src_ref=src,
            dst_ref=dst,
            send_sem=send_sem,
            recv_sem=recv_sem,
            device_id=where,
            device_id_type=MESH,
        )

    barrier = pltpu.get_barrier_semaphore()

    def greet(k, carry):
        peer = {"expert": lax.rem(me + k, holders)}
        pl.semaphore_signal(barrier, inc=1, device_id=peer, device_id_type=MESH)
        return carry

    lax.fori_loop(1, holders, greet, 0)
    for peer in (core, right, left, other):
        pl.semaphore_signal(barrier, inc=1, device_id=peer, device_id_type=MESH)
    own_got = [
        pltpu.make_async_copy(packed.at[kind, p, me], got.at[c, me], z_own.at[c])
        for c, (kind, p) in enumerate(chunks[:3])
    ]
    own_weights = [
        pltpu.make_async_copy(src.at[0], dst.at[0], w_own.at[i])
        for i, (src, dst) in enumerate(weights)
    ]
    for copy in own_got + own_weights:
        copy.start()
    pl.semaphore_wait(barrier, holders + 3)

    def to_all(send):
        def both_ways(k, carry):
            send(lax.rem(me + k, holders))
            send(lax.rem(me + holders - k, holders))
            return carry

        lax.fori_loop(1, holders // 2, both_ways, 0)
        send(lax.rem(me + holders // 2, holders))

    def dispatch(c):
        kind, p = chunks[c]

        def send(peer):
            remote(
                packed.at[kind, p, peer],
                got.at[c, me],
                z_send.at[c],
                z_recv.at[c],
                {"expert": peer},
            ).start()

        to_all(send)

    rest = pl.ds(0, holders - 1)

    def all_of(ref, sem):
        pltpu.make_async_copy(ref.at[rest], ref.at[rest], sem).wait()

    dispatch(0)
    given_weights = [
        remote(src.at[0], dst.at[1], w_send.at[i], w_recv.at[i], core)
        for i, (src, dst) in enumerate(weights)
    ]
    for copy in given_weights:
        copy.start()
    dispatch(1)

    def spread(c, which):
        kind, p = chunks[c]
        at = 2 * (q if which == 0 else 1 - q) + p
        src = rows.at[kind, 0, at]
        return tuple(
            remote(
                src,
                rows.at[kind, 1 + i, at],
                x_send.at[c, which, i],
                x_recv.at[c, which, i],
                where,
            )
            for i, where in ((0, right), (1, left))
        )

    def forward(c, which):
        kind, p = chunks[c]
        at = 2 * (q if which == 0 else 1 - q) + p
        return tuple(
            remote(
                rows.at[kind, 1 + i, at, part_of],
                rows.at[kind, 3, at, part_of],
                f_send.at[c, which, i],
                f_recv.at[c, which, i],
                where,
            )
            for i, part_of, where in ((0, upper, right), (1, lower, left))
        )

    swaps, spreads, forwards = [], {}, {}
    for c, (kind, p) in enumerate(chunks):
        mine = rows.at[kind, 0, 2 * q + p]
        swaps.append(remote(mine, mine, y_send.at[c], y_recv.at[c], pair))
        for which in range(1 if c < 2 else 2):
            spreads[c, which] = spread(c, which)
            forwards[c, which] = forward(c, which)

    def hand_over(c, source):
        kind, p = chunks[c]
        block = rows.at[kind, source, 2 * q + p]
        return remote(block, block, l_send.at[c, source - 1], l_recv.at[c, source - 1], pair)

    handed = {(c, source): hand_over(c, source) for c in range(2) for source in (1, 2, 3)}
    crossed = rows.at[0, 0, 2 * q + etp]
    cross = remote(crossed, crossed, o_sem.at[0], o_sem.at[1], other)

    def send_own(c):
        swaps[c].start()
        for copy in spreads[c, 0]:
            copy.start()

    def compact(c):
        kind, p = chunks[c]
        own_got[c].wait()
        all_of(got.at[c], z_recv.at[c])
        slots = got[c].reshape(2 * holders, quarter)
        dense = jnp.dot(collect[...], slots, preferred_element_type=f32)
        rows[kind, 0, 2 * q + p] = dense.astype(bf16)

    def send_pairs(c):
        swaps[c].wait_recv()
        for copy in spreads[c, 1]:
            copy.start()

    def pass_on(c, which):
        for arrive, copy in zip(spreads[c, which], forwards[c, which]):
            arrive.wait_recv()
            copy.start()

    def pass_and_hand(c):
        for i in range(2):
            spreads[c, 0][i].wait_recv()
            forwards[c, 0][i].start()
            handed[c, 1 + i].start()

    def hand_opposite(c):
        for copy in forwards[c, 0]:
            copy.wait_recv()
        handed[c, 3].start()

    def passed(c):
        for copy in forwards[c, 0] + forwards[c, 1]:
            copy.wait_recv()

    def times(kind, b, n, weight):
        total_of = jnp.zeros((n * count, weight.shape[0]), f32)
        for piece in range(4):
            a = rows[kind, pl.ds(b, n), piece].reshape(n * count, quarter)
            columns = weight[:, piece * quarter : (piece + 1) * quarter]
            total_of += lax.dot_general(a, columns, FLAT, preferred_element_type=f32)
        return total_of

    def first_products(b, n):
        def one(w, carry):
            gate_up[0, w, pl.ds(b * count, n * count)] = times(0, b, n, w_gate[w])
            gate_up[1, w, pl.ds(b * count, n * count)] = times(0, b, n, w_up[w])
            return carry

        lax.fori_loop(0, 2, one, 0)

    def hidden_grads(b, n):
        def one(w, carry):
            back = times(1, b, n, w_down[w])
            gate = gate_up[0, w, pl.ds(b * count, n * count)]
            up = gate_up[1, w, pl.ds(b * count, n * count)]
            s = jax.nn.sigmoid(gate)
            here = pl.ds(0, n * count)
            hidden[w, 0, here] = (back * up * s * (1.0 + gate * (1.0 - s))).astype(bf16)
            hidden[w, 1, here] = (back * gate * s).astype(bf16)
            return carry

        lax.fori_loop(0, 2, one, 0)

    def row_grads(b, n, piece):
        at = pl.ds(pl.multiple_of(piece * quarter, quarter), quarter)
        here = pl.ds(0, n * count)
        grad = jnp.zeros((n * count, quarter), f32)
        for w in range(2):
            for i, weight in enumerate((w_gate, w_up)):
                grad += jnp.dot(hidden[w, i, here], weight[w, :, at], preferred_element_type=f32)
        part[pl.ds(b, n), piece] = grad.reshape(n, count, quarter)

    def all_row_grads(b, n):
        def one(piece, carry):
            row_grads(b, n, piece)
            return carry

        lax.fori_loop(0, 4, one, 0)

    compact(0)
    cross.start()
    send_own(0)
    dispatch(2)
    pass_and_hand(0)
    compact(1)
    send_own(1)
    cross.wait_recv()
    send_own(3)
    hand_opposite(0)
    pass_and_hand(1)
    send_pairs(3)
    compact(2)
    send_own(2)
    pass_on(3, 0)
    hand_opposite(1)
    send_pairs(2)
    pass_on(2, 0)
    for copy in own_weights + given_weights:
        copy.wait()
    swaps[0].wait_recv()
    first_products(0, 1)
    pass_on(3, 1)
    handed[0, 1].wait_recv()
    handed[0, 2].wait_recv()
    first_products(1, 2)
    swaps[1].wait_recv()
    hidden_grads(0, 1)
    pass_on(2, 1)
    all_row_grads(0, 1)
    handed[0, 3].wait_recv()
    passed(3)
    first_products(3, 1)

    handed[1, 1].wait_recv()
    handed[1, 2].wait_recv()
    hidden_grads(1, 2)
    all_row_grads(1, 2)
    direct_out[0] = part[2, :, lower].astype(bf16)
    direct_out[1] = part[1, :, upper].astype(bf16)
    direct = [
        remote(direct_out.at[i], direct_in.at[i], d_send.at[i], d_recv.at[i], where)
        for i, where in ((0, right), (1, left))
    ]
    for copy in direct:
        copy.start()
    handed[1, 3].wait_recv()
    passed(2)
    hidden_grads(3, 1)

    order = (2 * (1 - etp) + 1 - q, 2 * (1 - etp) + q, 2 * etp + 1 - q, 2 * etp + q)
    relays, sums = [], []
    for stage, piece in enumerate(order):
        row_grads(3, 1, piece)
        for i, part_of, where in ((0, upper, right), (1, lower, left)):
            relay_out[i, stage] = part[3, piece, part_of].astype(bf16)
            relays.append(
                remote(
                    relay_out.at[i, stage],
                    relay_in.at[i, stage],
                    r_send.at[i, stage],
                    r_recv.at[i, stage],
                    where,
                )
            )
            relays[-1].start()
    for stage, piece in enumerate(order):
        for i, b, part_of, where in ((0, 2, upper, right), (1, 1, lower, left)):
            relays[2 * stage + i].wait_recv()
            added = part[b, piece, part_of] + relay_in[i, stage].astype(f32)
            sum_out[i, stage] = added.astype(bf16)
            sums.append(
                remote(
                    sum_out.at[i, stage],
                    sum_in.at[i, stage],
                    s_send.at[i, stage],
                    s_recv.at[i, stage],
                    where,
                )
            )
            sums[-1].start()
    for copy in direct:
        copy.wait_recv()

    def along_x(stage):
        piece = order[stage]
        pieces = []
        for i, part_of in ((0, upper), (1, lower)):
            sums[2 * stage + i].wait_recv()
            terms = sum_in[i, stage].astype(f32) + direct_in[1 - i, piece].astype(f32)
            pieces.append((part[0, piece, part_of] + terms) * gain[part_of, :])
        return jnp.concatenate(pieces, axis=0)

    pair_swaps = [
        remote(pair_out.at[i], pair_in.at[i], p_send.at[i], p_recv.at[i], pair) for i in range(2)
    ]
    pair_out[0] = along_x(0).astype(bf16)
    pair_swaps[0].start()
    total[...] = along_x(1)
    pair_swaps[0].wait_recv()
    half_out[...] = (total[...] + pair_in[0].astype(f32)).astype(bf16)
    half_swap = remote(half_out, half_in, h_sem.at[0], h_sem.at[1], other)
    half_swap.start()
    pair_out[1] = along_x(2).astype(bf16)
    pair_swaps[1].start()
    total[...] = along_x(3)
    pair_swaps[1].wait_recv()
    total[...] += pair_in[1].astype(f32)
    half_swap.wait_recv()
    result = (total[...] + half_in[...].astype(f32)).astype(bf16)

    slots = jnp.dot(collect_t[...], result, preferred_element_type=f32).astype(bf16)
    returned[...] = slots.reshape(holders, 2, quarter)
    own_back = pltpu.make_async_copy(returned.at[me], arrived.at[me], b_sem.at[2])
    own_back.start()

    def send_back(peer):
        remote(
            returned.at[peer], arrived.at[me], b_sem.at[0], b_sem.at[1], {"expert": peer}
        ).start()

    to_all(send_back)
    own_back.wait()
    all_of(returned, b_sem.at[0])
    for c, (kind, p) in enumerate(chunks[:3]):
        all_of(packed.at[kind, p], z_send.at[c])
    copies = swaps + direct + relays + sums + pair_swaps + [cross, half_swap]
    copies += list(handed.values())
    for key in spreads:
        copies += spreads[key] + forwards[key]
    for copy in copies:
        copy.wait_send()
    all_of(arrived, b_sem.at[1])


def layer(n_dp, packed, collect, gain, gate, up, down):
    holders, most_slots, quarter = packed.shape[2:]
    count = collect.shape[0]
    slice_width = gate.shape[1]
    bf16, f32 = jnp.bfloat16, jnp.float32
    any_spec = pl.BlockSpec(memory_space=pl.ANY)
    vmem_spec = pl.BlockSpec(memory_space=pltpu.VMEM)
    slices = pltpu.VMEM((2, slice_width, 4 * quarter), bf16)
    half_rows = pltpu.VMEM((2, 4, count // 2, quarter), bf16)
    two_quarters = pltpu.VMEM((2, count, quarter), bf16)
    one_quarter = pltpu.VMEM((count, quarter), bf16)
    return pl.pallas_call(
        functools.partial(layer_kernel, n_dp),
        out_shape=jax.ShapeDtypeStruct((holders, most_slots, quarter), bf16),
        in_specs=[any_spec, vmem_spec, vmem_spec, vmem_spec, any_spec, any_spec, any_spec],
        out_specs=any_spec,
        scratch_shapes=[
            pltpu.VMEM((3, holders, most_slots, quarter), bf16),
            pltpu.VMEM((2, 4, 4, count, quarter), bf16),
            slices,
            slices,
            slices,
            pltpu.VMEM((2, 2, 4 * count, slice_width), f32),
            pltpu.VMEM((2, 2, 2 * count, slice_width), bf16),
            pltpu.VMEM((4, 4, count, quarter), f32),
            pltpu.VMEM((count, quarter), f32),
            half_rows,
            half_rows,
            half_rows,
            half_rows,
            half_rows,
            half_rows,
            two_quarters,
            two_quarters,
            one_quarter,
            one_quarter,
            pltpu.VMEM((holders, most_slots, quarter), bf16),
            SEM((3,)),
            SEM((3,)),
            SEM((3,)),
            SEM((3,)),
            SEM((3,)),
            SEM((3,)),
            SEM((4,)),
            SEM((4,)),
            SEM((2,)),
            SEM((2, 3)),
            SEM((2, 3)),
            SEM((4, 2, 2)),
            SEM((4, 2, 2)),
            SEM((4, 2, 2)),
            SEM((4, 2, 2)),
            SEM((2,)),
            SEM((2,)),
            SEM((2, 4)),
            SEM((2, 4)),
            SEM((2, 4)),
            SEM((2, 4)),
            SEM((2,)),
            SEM((2,)),
            SEM((2,)),
            SEM((3,)),
        ],
        compiler_params=pltpu.CompilerParams(
            collective_id=0, has_side_effects=True, vmem_limit_bytes=40 * 1024 * 1024
        ),
    )(packed, collect, collect.T, gain, gate, up, down)


def body(tokens, cotangent, scores, chosen, w_gate, w_up, w_down):
    local_rows, model_width = tokens.shape
    experts = chosen.shape[1]
    capacity = chosen.shape[2]
    holders = lax.axis_size("expert")
    most_slots = 2 * ((local_rows + experts - 1) // experts)
    holder_index = lax.axis_index("expert")
    expert_id = holder_index // 2
    pick_table = chosen[0]
    holder_of = pick_table // local_rows
    positions = jnp.arange(capacity, dtype=jnp.int32)
    slot_range = jnp.arange(most_slots, dtype=jnp.int32)
    first_slot = jnp.sum((holder_of < holder_index).astype(jnp.int32), axis=1, keepdims=True)
    slot_index = positions[None, :] - first_slot
    is_mine = holder_of == holder_index
    pick_slot = (
        is_mine[:, :, None] & (slot_index[:, :, None] == slot_range[None, None, :])
    ).astype(jnp.bfloat16)
    local_index = pick_table - holder_index * local_rows
    pick_token = (
        local_index[:, :, None] == jnp.arange(local_rows, dtype=jnp.int32)[None, None, :]
    ).astype(jnp.bfloat16)
    sender = jnp.einsum(
        "ecj,eck->ejk", pick_slot, pick_token, preferred_element_type=jnp.float32
    ).astype(jnp.bfloat16)
    own_list = lax.dynamic_index_in_dim(pick_table, expert_id, 0, keepdims=False)
    own_holder = own_list // local_rows
    ahead_count = jnp.sum((own_holder[None, :] < own_holder[:, None]).astype(jnp.int32), axis=1)
    own_slot = positions - ahead_count
    holder_range = jnp.arange(holders, dtype=jnp.int32)
    collect = (
        (own_holder[:, None, None] == holder_range[None, :, None])
        & (own_slot[:, None, None] == slot_range[None, None, :])
    ).astype(jnp.bfloat16)
    gain = lax.dynamic_index_in_dim(scores[0], expert_id, 0, keepdims=False)[:, None]

    stacked = jnp.stack([tokens, cotangent]).reshape(2, local_rows, 2, 2, model_width // 4)
    packed = jnp.einsum(
        "ejk,akqpd->apeqjd", sender, stacked, preferred_element_type=jnp.float32
    ).astype(jnp.bfloat16)
    arrived = layer(
        lax.axis_size("dp"),
        packed.reshape(2, 2, holders, most_slots, model_width // 4),
        collect.reshape(capacity, holders * most_slots),
        gain,
        jnp.swapaxes(w_gate, 1, 2),
        jnp.swapaxes(w_up, 1, 2),
        w_down,
    ).reshape(experts, 2, most_slots, model_width // 4)
    grad_tokens = jnp.einsum(
        "ejk,eqjd->kqd", sender, arrived, preferred_element_type=jnp.float32
    )
    return grad_tokens.reshape(local_rows, model_width // 2).astype(jnp.bfloat16)


def solution(mesh):
    placed = (
        P(("dp", "expert"), None),
        P(("dp", "expert"), None),
        P("dp", None, None),
        P("dp", None, None),
        P("expert", None, ("dp", "etp")),
        P("expert", None, ("dp", "etp")),
        P("expert", ("dp", "etp"), None),
    )
    return jax.shard_map(
        body, mesh=mesh, in_specs=placed, out_specs=P(("dp", "expert"), "etp"), check_vma=False
    )
```

```python
import functools

import jax
import jax.numpy as jnp
from jax import lax
from jax.experimental import pallas as pl
from jax.experimental.pallas import tpu as pltpu
from jax.sharding import PartitionSpec as P

MESH = pl.DeviceIdType.MESH
SEM = pltpu.SemaphoreType.DMA
FLAT = (((1,), (1,)), ((), ()))


def layer_kernel(
    n_dp,
    packed_tokens,
    packed_grads,
    collect,
    collect_t,
    gain,
    gate_in,
    up_in,
    down_in,
    arrived,
    got,
    rows,
    w_gate,
    w_up,
    w_down,
    gate_up,
    hidden,
    part,
    total,
    direct_out,
    direct_in,
    relay_out,
    relay_in,
    sum_out,
    sum_in,
    pair_out,
    pair_in,
    half_out,
    half_in,
    returned,
    z_send,
    z_recv,
    z_own,
    w_own,
    w_send,
    w_recv,
    y_send,
    y_recv,
    x_send,
    x_recv,
    f_send,
    f_recv,
    d_send,
    d_recv,
    r_send,
    r_recv,
    s_send,
    s_recv,
    p_sem,
    h_sem,
    b_sem,
):
    holders = arrived.shape[0]
    count = rows.shape[3]
    half = rows.shape[4]
    quarter = half // 2
    bf16, f32 = jnp.bfloat16, jnp.float32
    dp = lax.axis_index("dp")
    me = lax.axis_index("expert")
    etp = lax.axis_index("etp")
    q = lax.rem(me, 2)
    core = {"dp": dp + 1 - 2 * lax.rem(dp, 2)}
    right = {"dp": lax.rem(dp + 2, n_dp)}
    left = {"dp": lax.rem(dp + n_dp - 2, n_dp)}
    pair = {"expert": me + 1 - 2 * q}
    other = {"etp": 1 - etp}
    packed = (packed_tokens, packed_grads)
    weights = ((gate_in, w_gate), (up_in, w_up), (down_in, w_down))

    def remote(src, dst, send_sem, recv_sem, where):
        return pltpu.make_async_remote_copy(
            src_ref=src,
            dst_ref=dst,
            send_sem=send_sem,
            recv_sem=recv_sem,
            device_id=where,
            device_id_type=MESH,
        )

    barrier = pltpu.get_barrier_semaphore()

    def greet(k, carry):
        peer = {"expert": lax.rem(me + k, holders)}
        pl.semaphore_signal(barrier, inc=1, device_id=peer, device_id_type=MESH)
        return carry

    lax.fori_loop(1, holders, greet, 0)
    for peer in (core, right, left, other):
        pl.semaphore_signal(barrier, inc=1, device_id=peer, device_id_type=MESH)
    own_got = [
        pltpu.make_async_copy(packed[kind].at[me], got.at[kind, me], z_own.at[kind])
        for kind in range(2)
    ]
    own_weights = [
        pltpu.make_async_copy(src.at[0], dst.at[0], w_own.at[i])
        for i, (src, dst) in enumerate(weights)
    ]
    for copy in own_got + own_weights:
        copy.start()
    pl.semaphore_wait(barrier, holders + 3)

    def to_all(send):
        def both_ways(k, carry):
            send(lax.rem(me + k, holders))
            send(lax.rem(me + holders - k, holders))
            return carry

        lax.fori_loop(1, holders // 2, both_ways, 0)
        send(lax.rem(me + holders // 2, holders))

    def dispatch(kind):
        def send(peer):
            remote(
                packed[kind].at[peer],
                got.at[kind, me],
                z_send.at[kind],
                z_recv.at[kind],
                {"expert": peer},
            ).start()

        to_all(send)

    rest = pl.ds(0, holders - 1)

    def all_of(ref, sem):
        pltpu.make_async_copy(ref.at[rest], ref.at[rest], sem).wait()

    dispatch(0)
    given_weights = [
        remote(src.at[0], dst.at[1], w_send.at[i], w_recv.at[i], core)
        for i, (src, dst) in enumerate(weights)
    ]
    dispatch(1)

    def spread(kind, side):
        src = rows.at[kind, 0, side]
        return (
            remote(
                src,
                rows.at[kind, 1, side],
                x_send.at[kind, side, 0],
                x_recv.at[kind, side, 0],
                right,
            ),
            remote(
                src,
                rows.at[kind, 2, side],
                x_send.at[kind, side, 1],
                x_recv.at[kind, side, 1],
                left,
            ),
        )

    def forward(kind, side):
        upper, lower = pl.ds(0, count // 2), pl.ds(count // 2, count // 2)
        return (
            remote(
                rows.at[kind, 1, side, upper],
                rows.at[kind, 3, side, upper],
                f_send.at[kind, side, 0],
                f_recv.at[kind, side, 0],
                right,
            ),
            remote(
                rows.at[kind, 2, side, lower],
                rows.at[kind, 3, side, lower],
                f_send.at[kind, side, 1],
                f_recv.at[kind, side, 1],
                left,
            ),
        )

    swaps, spreads, forwards = [], {}, {}
    for kind in range(2):
        swaps.append(
            remote(
                rows.at[kind, 0, q], rows.at[kind, 0, q], y_send.at[kind], y_recv.at[kind], pair
            )
        )
        for which, side in ((0, q), (1, 1 - q)):
            spreads[kind, which] = spread(kind, side)
            forwards[kind, which] = forward(kind, side)

    def compact(kind):
        own_got[kind].wait()
        all_of(got.at[kind], z_recv.at[kind])
        slots = got[kind].reshape(2 * holders, half)
        rows[kind, 0, q] = jnp.dot(collect[...], slots, preferred_element_type=f32).astype(bf16)
        swaps[kind].start()
        for copy in spreads[kind, 0]:
            copy.start()

    def pass_on(kind, which):
        for arrive, copy in zip(spreads[kind, which], forwards[kind, which]):
            arrive.wait_recv()
            copy.start()

    def times(kind, b, n, weight):
        a = rows[kind, pl.ds(b, n), 0].reshape(n * count, half)
        c = rows[kind, pl.ds(b, n), 1].reshape(n * count, half)
        return lax.dot_general(
            a, weight[:, :half], FLAT, preferred_element_type=f32
        ) + lax.dot_general(c, weight[:, half:], FLAT, preferred_element_type=f32)

    def first_products(b, n):
        def one(w, carry):
            gate_up[0, w, pl.ds(b * count, n * count)] = times(0, b, n, w_gate[w])
            gate_up[1, w, pl.ds(b * count, n * count)] = times(0, b, n, w_up[w])
            return carry

        lax.fori_loop(0, 2, one, 0)

    def hidden_grads(b, n):
        def one(w, carry):
            back = times(1, b, n, w_down[w])
            gate = gate_up[0, w, pl.ds(b * count, n * count)]
            up = gate_up[1, w, pl.ds(b * count, n * count)]
            s = jax.nn.sigmoid(gate)
            here = pl.ds(0, n * count)
            hidden[w, 0, here] = (back * up * s * (1.0 + gate * (1.0 - s))).astype(bf16)
            hidden[w, 1, here] = (back * gate * s).astype(bf16)
            return carry

        lax.fori_loop(0, 2, one, 0)

    def row_grads(b, n, piece):
        at = pl.ds(pl.multiple_of(piece * quarter, quarter), quarter)
        here = pl.ds(0, n * count)
        grad = jnp.zeros((n * count, quarter), f32)
        for w in range(2):
            for i, weight in enumerate((w_gate, w_up)):
                grad += jnp.dot(hidden[w, i, here], weight[w, :, at], preferred_element_type=f32)
        part[pl.ds(b, n), piece] = grad.reshape(n, count, quarter)

    def all_row_grads(b, n):
        def one(piece, carry):
            row_grads(b, n, piece)
            return carry

        lax.fori_loop(0, 4, one, 0)

    compact(0)
    for copy in given_weights:
        copy.start()
    swaps[0].wait_recv()
    for copy in spreads[0, 1]:
        copy.start()
    pass_on(0, 0)
    compact(1)
    pass_on(0, 1)
    for copy in own_weights + given_weights:
        copy.wait()
    first_products(0, 1)
    first_products(1, 2)
    swaps[1].wait_recv()
    for copy in spreads[1, 1]:
        copy.start()
    pass_on(1, 0)
    for copy in forwards[0, 0] + forwards[0, 1]:
        copy.wait_recv()
    first_products(3, 1)
    hidden_grads(0, 1)
    all_row_grads(0, 1)
    pass_on(1, 1)

    hidden_grads(1, 2)
    all_row_grads(1, 2)
    for piece in range(2):
        direct_out[0, piece] = part[2, 2 + piece].astype(bf16)
        direct_out[1, piece] = part[1, piece].astype(bf16)
    direct = [
        remote(direct_out.at[i], direct_in.at[i], d_send.at[i], d_recv.at[i], where)
        for i, where in ((0, right), (1, left))
    ]
    for copy in direct:
        copy.start()
    for copy in forwards[1, 0] + forwards[1, 1]:
        copy.wait_recv()
    hidden_grads(3, 1)

    relays, sums = [], []
    for stage, sub in ((0, 1 - q), (1, q)):
        for i, piece, where in ((0, sub, right), (1, 2 + sub, left)):
            row_grads(3, 1, piece)
            relay_out[i, stage] = part[3, piece].astype(bf16)
            relays.append(
                remote(
                    relay_out.at[i, stage],
                    relay_in.at[i, stage],
                    r_send.at[i, stage],
                    r_recv.at[i, stage],
                    where,
                )
            )
            relays[-1].start()
    for stage, sub in ((0, 1 - q), (1, q)):
        for i, b, piece, where in ((0, 2, sub, right), (1, 1, 2 + sub, left)):
            relays[2 * stage + i].wait_recv()
            sum_out[i, stage] = (part[b, piece] + relay_in[i, stage].astype(f32)).astype(bf16)
            sums.append(
                remote(
                    sum_out.at[i, stage],
                    sum_in.at[i, stage],
                    s_send.at[i, stage],
                    s_recv.at[i, stage],
                    where,
                )
            )
            sums[-1].start()
    for copy in direct:
        copy.wait_recv()
    weight = gain[...]

    def along_x(stage, sub, i):
        sums[2 * stage + i].wait_recv()
        terms = sum_in[i, stage].astype(f32) + direct_in[1 - i, sub].astype(f32)
        return (part[0, 2 * i + sub] + terms) * weight

    for i in range(2):
        pair_out[i] = along_x(0, 1 - q, i).astype(bf16)
    pair_swap = remote(pair_out, pair_in, p_sem.at[0], p_sem.at[1], pair)
    pair_swap.start()
    for i in range(2):
        total[i] = along_x(1, q, i)
    pair_swap.wait_recv()
    half_out[...] = (total[1 - etp] + pair_in[1 - etp].astype(f32)).astype(bf16)
    half_swap = remote(half_out, half_in, h_sem.at[0], h_sem.at[1], other)
    half_swap.start()
    mine = total[etp] + pair_in[etp].astype(f32)
    half_swap.wait_recv()
    result = (mine + half_in[...].astype(f32)).astype(bf16)

    slots = jnp.dot(collect_t[...], result, preferred_element_type=f32).astype(bf16)
    returned[...] = slots.reshape(holders, 2, quarter)
    own_back = pltpu.make_async_copy(returned.at[me], arrived.at[me], b_sem.at[2])
    own_back.start()

    def send_back(peer):
        remote(
            returned.at[peer], arrived.at[me], b_sem.at[0], b_sem.at[1], {"expert": peer}
        ).start()

    to_all(send_back)
    own_back.wait()
    all_of(returned, b_sem.at[0])
    for kind in range(2):
        all_of(packed[kind], z_send.at[kind])
    copies = swaps + direct + relays + sums + [pair_swap, half_swap]
    for key in spreads:
        copies += spreads[key] + forwards[key]
    for copy in copies:
        copy.wait_send()
    all_of(arrived, b_sem.at[1])


def layer(n_dp, packed_tokens, packed_grads, collect, gain, gate, up, down):
    holders, most_slots, half = packed_tokens.shape
    count = collect.shape[0]
    quarter = half // 2
    slice_width = gate.shape[1]
    bf16, f32 = jnp.bfloat16, jnp.float32
    any_spec = pl.BlockSpec(memory_space=pl.ANY)
    vmem_spec = pl.BlockSpec(memory_space=pltpu.VMEM)
    slices = pltpu.VMEM((2, slice_width, 2 * half), bf16)
    quarters = pltpu.VMEM((2, 2, count, quarter), bf16)
    two_quarters = pltpu.VMEM((2, count, quarter), bf16)
    one_quarter = pltpu.VMEM((count, quarter), bf16)
    return pl.pallas_call(
        functools.partial(layer_kernel, n_dp),
        out_shape=jax.ShapeDtypeStruct((holders, most_slots, quarter), bf16),
        in_specs=[any_spec, any_spec, vmem_spec, vmem_spec, vmem_spec, any_spec, any_spec, any_spec],
        out_specs=any_spec,
        scratch_shapes=[
            pltpu.VMEM((2, holders, most_slots, half), bf16),
            pltpu.VMEM((2, 4, 2, count, half), bf16),
            slices,
            slices,
            slices,
            pltpu.VMEM((2, 2, 4 * count, slice_width), f32),
            pltpu.VMEM((2, 2, 2 * count, slice_width), bf16),
            pltpu.VMEM((4, 4, count, quarter), f32),
            pltpu.VMEM((2, count, quarter), f32),
            quarters,
            quarters,
            quarters,
            quarters,
            quarters,
            quarters,
            two_quarters,
            two_quarters,
            one_quarter,
            one_quarter,
            pltpu.VMEM((holders, most_slots, quarter), bf16),
            SEM((2,)),
            SEM((2,)),
            SEM((2,)),
            SEM((3,)),
            SEM((3,)),
            SEM((3,)),
            SEM((2,)),
            SEM((2,)),
            SEM((2, 2, 2)),
            SEM((2, 2, 2)),
            SEM((2, 2, 2)),
            SEM((2, 2, 2)),
            SEM((2,)),
            SEM((2,)),
            SEM((2, 2)),
            SEM((2, 2)),
            SEM((2, 2)),
            SEM((2, 2)),
            SEM((2,)),
            SEM((2,)),
            SEM((3,)),
        ],
        compiler_params=pltpu.CompilerParams(
            collective_id=0, has_side_effects=True, vmem_limit_bytes=40 * 1024 * 1024
        ),
    )(packed_tokens, packed_grads, collect, collect.T, gain, gate, up, down)


def body(tokens, cotangent, scores, chosen, w_gate, w_up, w_down):
    local_rows, model_width = tokens.shape
    experts = chosen.shape[1]
    capacity = chosen.shape[2]
    holders = lax.axis_size("expert")
    most_slots = 2 * ((local_rows + experts - 1) // experts)
    holder_index = lax.axis_index("expert")
    expert_id = holder_index // 2
    pick_table = chosen[0]
    holder_of = pick_table // local_rows
    positions = jnp.arange(capacity, dtype=jnp.int32)
    slot_range = jnp.arange(most_slots, dtype=jnp.int32)
    first_slot = jnp.sum((holder_of < holder_index).astype(jnp.int32), axis=1, keepdims=True)
    slot_index = positions[None, :] - first_slot
    is_mine = holder_of == holder_index
    pick_slot = (
        is_mine[:, :, None] & (slot_index[:, :, None] == slot_range[None, None, :])
    ).astype(jnp.bfloat16)
    local_index = pick_table - holder_index * local_rows
    pick_token = (
        local_index[:, :, None] == jnp.arange(local_rows, dtype=jnp.int32)[None, None, :]
    ).astype(jnp.bfloat16)
    sender = jnp.einsum(
        "ecj,eck->ejk", pick_slot, pick_token, preferred_element_type=jnp.float32
    ).astype(jnp.bfloat16)
    own_list = lax.dynamic_index_in_dim(pick_table, expert_id, 0, keepdims=False)
    own_holder = own_list // local_rows
    ahead_count = jnp.sum((own_holder[None, :] < own_holder[:, None]).astype(jnp.int32), axis=1)
    own_slot = positions - ahead_count
    holder_range = jnp.arange(holders, dtype=jnp.int32)
    collect = (
        (own_holder[:, None, None] == holder_range[None, :, None])
        & (own_slot[:, None, None] == slot_range[None, None, :])
    ).astype(jnp.bfloat16)
    gain = lax.dynamic_index_in_dim(scores[0], expert_id, 0, keepdims=False)[:, None]

    def pack(values):
        sent = jnp.einsum(
            "ejk,kqd->eqjd",
            sender,
            values.reshape(local_rows, 2, model_width // 2),
            preferred_element_type=jnp.float32,
        ).astype(jnp.bfloat16)
        return sent.reshape(holders, most_slots, model_width // 2)

    arrived = layer(
        lax.axis_size("dp"),
        pack(tokens),
        pack(cotangent),
        collect.reshape(capacity, holders * most_slots),
        gain,
        jnp.swapaxes(w_gate, 1, 2),
        jnp.swapaxes(w_up, 1, 2),
        w_down,
    ).reshape(experts, 2, most_slots, model_width // 4)
    grad_tokens = jnp.einsum(
        "ejk,eqjd->kqd", sender, arrived, preferred_element_type=jnp.float32
    )
    return grad_tokens.reshape(local_rows, model_width // 2).astype(jnp.bfloat16)


def solution(mesh):
    placed = (
        P(("dp", "expert"), None),
        P(("dp", "expert"), None),
        P("dp", None, None),
        P("dp", None, None),
        P("expert", None, ("dp", "etp")),
        P("expert", None, ("dp", "etp")),
        P("expert", ("dp", "etp"), None),
    )
    return jax.shard_map(
        body, mesh=mesh, in_specs=placed, out_specs=P(("dp", "expert"), "etp"), check_vma=False
    )
```
